32 devices in a mesh: prow: 4 (over y, x), pcol: 8 (over z, core).
Axes of the slice: x: 2, y: 2, z: 4, core: 2. Of those that a mesh axis runs over, the one named last changes fastest.
Arguments:
- inverse_matrix: float32 [12288, 12288], P('prow', 'pcol'), may hold values from -6 to 6
- factor_blocks: float32 [4, 48, 256, 256], P(None, 'prow', 'pcol'), may hold values from -0.0546875 to 0.0546875
- factor_inverse: float32 [4, 256, 256], replicated, may hold values from -8 to 8, as said below
- diag_given: float32 [4, 256, 256], replicated, may hold values from -6 to 6
- block_lists: int32 [4, 48], replicated, may hold values from 0 to 47, as said below
- list_mask: int32 [4, 48], replicated, may hold values from 0 to 1, as said below
- slot_of_block: int32 [48], replicated, may hold values from 0 to 47, as said below
Outputs:
- panel_inverse: float32 [4, 48, 256, 256], P(None, 'prow', 'pcol')
- diag_inverse: float32 [4, 256, 256], replicated
The draws below stay inside these ranges and needn't reach their ends.
Inputs may be any that keep to these rules, and one draw needn't show every extreme that they name: `block_lists`: each panel's list names every block of the window once; entries with mask 0 are padding. `list_mask`: 1 marks a used list entry; for every k, of the 48 pairs (p, s) with s // 12 = k, exactly 36 have slot_valid[p, s] = 1. `slot_of_block`: a permutation of the 48 slots. `factor_inverse`: lower triangular with a positive diagonal.
All inputs are finite; a program needn't handle non-finite values.
Results may differ from the reference program's by a relative error of at most 0.00007.
Values sent between devices are 32-bit elements; how exact they have to be, the bound alone decides.
No kernel may reach another device: no remote copies, remote signals or barrier semaphores. Data moves between devices by JAX's collectives and lax.ppermute only.
A program may use at most 128 MiB of HBM per device.

```python
import math
import jax
import jax.numpy as jnp
from jax import lax

B = 256
P_SIZE = 4
NB = 48
RBLK = 12
KEEP = 36


def draw_factor_inverse(key, part):
    key_diag = jax.random.fold_in(key, 11)
    key_lower = jax.random.fold_in(key, 12)
    diagonal = jnp.exp(jax.random.uniform(key_diag, (P_SIZE, B), jnp.float32, math.log(0.5), math.log(2.0)))
    lower_part = jnp.clip(jax.random.normal(key_lower, (P_SIZE, B, B), jnp.float32), -4.0, 4.0) / math.sqrt(B)
    identity = jnp.eye(B, dtype=jnp.float32)
    return jnp.tril(lower_part, -1) + diagonal[:, :, None] * identity[None, :, :]


def window_lists(key):
    key_slots = jax.random.fold_in(key, 21)
    key_lists = jax.random.fold_in(key, 22)
    key_valid = jax.random.fold_in(key, 23)
    slot_table = jax.random.permutation(key_slots, jnp.arange(NB, dtype=jnp.int32)).astype(jnp.int32)
    list_keys = jax.random.split(key_lists, P_SIZE)
    lists = jax.vmap(lambda one: jax.random.permutation(one, jnp.arange(NB, dtype=jnp.int32)))(list_keys).astype(jnp.int32)
    group_keys = jax.random.split(key_valid, NB // RBLK)
    ranks = jax.vmap(lambda one: jax.random.permutation(one, jnp.arange(P_SIZE * RBLK, dtype=jnp.int32)))(group_keys)
    used = (ranks < KEEP).astype(jnp.int32).reshape(NB // RBLK, P_SIZE, RBLK)
    used = jnp.transpose(used, (1, 0, 2)).reshape(P_SIZE, NB)
    slots = slot_table[lists]
    masks = jnp.take_along_axis(used, slots, axis=1).astype(jnp.int32)
    return (lists, masks, slot_table)


def draw_block_lists(key, part):
    return window_lists(key)[0]


def draw_list_mask(key, part):
    return window_lists(key)[1]


def draw_slot_of_block(key, part):
    return window_lists(key)[2]


def steps_of(stream_key, extent, shards, low, top_value):
    def one(axis_at, parts):
        draws = jax.random.uniform(jax.random.fold_in(jax.random.fold_in(stream_key, 6), axis_at), (parts,), jnp.float32, low / len(shards), top_value / len(shards))
        return jnp.repeat(jnp.exp(draws), extent[axis_at] // parts).reshape((-1,) + (1,) * (len(extent) - axis_at - 1))

    gain = one(*shards[0])
    for cut in shards[1:]:
        gain = gain * one(*cut)
    return gain


def bell_draw(stream_key, dims, scale, reach, cuts=(), held_as=jnp.bfloat16):
    loudness = steps_of(stream_key, dims, cuts, -0.22, 0.18) if cuts else 1.0
    entries = jax.random.normal(stream_key, dims, jnp.float32) * scale * loudness
    return jnp.minimum(jnp.maximum(entries, -reach), reach).astype(held_as)


def setup_inputs(seed: int = 0) -> dict:
    keys = jax.random.split(jax.random.key(seed), 8)
    return {
        "inverse_matrix": bell_draw(keys[0], (NB * B, NB * B), 1.0, 6.0, ((0, 4), (1, 8)), jnp.float32),
        "factor_blocks": bell_draw(keys[1], (P_SIZE, NB, B, B), ((NB * B) ** -0.5), 0.0546875, ((1, 4), (2, 8)), jnp.float32),
        "factor_inverse": draw_factor_inverse(jax.random.fold_in(keys[7], 71), 0),
        "diag_given": bell_draw(keys[3], (P_SIZE, B, B), 1.0, 6.0, (), jnp.float32),
        "block_lists": draw_block_lists(jax.random.fold_in(keys[7], 71), 0),
        "list_mask": draw_list_mask(jax.random.fold_in(keys[7], 71), 0),
        "slot_of_block": draw_slot_of_block(jax.random.fold_in(keys[7], 71), 0),
    }


def valid_slots(block_lists, list_mask, slot_of_block):
    window_blocks = block_lists.shape[1]
    block_ids = jnp.arange(window_blocks, dtype=jnp.int32)
    chosen = (block_lists[:, :, None] == block_ids[None, None, :]).astype(jnp.int32)
    slot_ids = jnp.sum(chosen * slot_of_block[None, None, :], axis=2).astype(jnp.int32)
    matches = (slot_ids[:, :, None] == block_ids[None, None, :]).astype(jnp.int32) * list_mask[:, :, None]
    return jnp.sum(matches, axis=1).astype(jnp.int32)


def reference(inverse_matrix, factor_blocks, factor_inverse, diag_given, block_lists, list_mask, slot_of_block):
    highest = lax.Precision.HIGHEST
    slot_valid = valid_slots(block_lists, list_mask, slot_of_block).astype(jnp.float32)
    normalized = jnp.einsum("psij,pjk->psik", factor_blocks, factor_inverse, precision=highest)
    normalized = normalized * slot_valid[:, :, None, None]
    panel_width = factor_inverse.shape[1]
    window_blocks = block_lists.shape[1]

    def one_panel(operands):
        normal_hat, valid_rows = operands
        column_stack = normal_hat.reshape(window_blocks * panel_width, panel_width)
        product = jnp.dot(inverse_matrix, column_stack, precision=highest, preferred_element_type=jnp.float32)
        return -(product.reshape(window_blocks, panel_width, panel_width) * valid_rows[:, None, None])

    panel_inverse = lax.map(one_panel, (normalized, slot_valid))
    diag_inverse = diag_given - jnp.einsum("psik,psil->pkl", normalized, panel_inverse, precision=highest)
    return panel_inverse, diag_inverse
```

```python
import functools
import math
import jax
import jax.numpy as jnp
from jax import lax
from jax.experimental import pallas as pl
from jax.experimental.pallas import tpu as pltpu
from jax.sharding import PartitionSpec as P

AXES = ("prow", "pcol")
HIGHEST = lax.Precision.HIGHEST
VMEM_LIMIT = 56 * 1024 * 1024


def whole(memory_space=pltpu.VMEM):
    return pl.BlockSpec(memory_space=memory_space)


def call(kernel, outs, scratch=(), n_scalar=1, n_in=1, flops=0, moved=0):
    return pl.pallas_call(
        kernel,
        out_shape=outs,
        in_specs=[whole(pltpu.SMEM)] * n_scalar + [whole()] * n_in,
        out_specs=jax.tree.map(lambda _: whole(), outs),
        scratch_shapes=list(scratch),
        compiler_params=pltpu.CompilerParams(vmem_limit_bytes=VMEM_LIMIT),
        cost_estimate=pl.CostEstimate(flops=flops, bytes_accessed=moved, transcendentals=0),
    )


def valid_slots(block_lists, list_mask, slot_of_block):
    window_blocks = block_lists.shape[1]
    block_ids = jnp.arange(window_blocks, dtype=jnp.int32)
    chosen = (block_lists[:, :, None] == block_ids[None, None, :]).astype(jnp.int32)
    slot_ids = jnp.sum(chosen * slot_of_block[None, None, :], axis=2)
    matches = (slot_ids[:, :, None] == block_ids[None, None, :]).astype(jnp.int32)
    return jnp.sum(matches * list_mask[:, :, None], axis=1)


def normalize_kernel(groups, lines, place, valid, f_ref, inv_ref, n_ref, *rest):
    panels, slots, rb, width = f_ref.shape
    halves = slots // 2
    scratch = rest[-len(groups):]
    outs = rest[: -len(groups)]
    r = place[0]
    for g, group in enumerate(groups):
        for at, p in enumerate(group):
            block = jnp.dot(
                f_ref[p].reshape(slots * rb, width), inv_ref[p],
                precision=HIGHEST, preferred_element_type=jnp.float32,
            )
            for s in range(slots):
                used = valid[p * slots + s] > 0
                one = jnp.where(used, block[s * rb : (s + 1) * rb], 0.0)
                n_ref[p, s] = one
                row = (at * halves + s % halves) * rb
                scratch[g][s // halves, row : row + rb] = one
        n = len(group) * halves * rb // lines
        for d in range(lines):
            start = pl.multiple_of((r ^ d) * n, 8)
            outs[g * lines + d][...] = scratch[g][:, pl.ds(start, n), :]


def to_planes_kernel(lines, place, *refs):
    r, z = place[0], place[1]
    for m in range(lines):
        which = r ^ ((z + m) % lines)
        for d in range(lines):

            @pl.when(which == d)
            def _(m=m, d=d):
                refs[lines + m][...] = refs[d][...]


def by_core_kernel(lines, place, *refs):
    h = place[2]
    mine, other = refs[lines:]
    for m in range(lines):
        mine[m] = refs[m][h]
        other[m] = refs[m][1 - h]


def assemble_kernel(lines, rb, place, *refs):
    pieces = refs[: 2 * lines]
    hi_ref, lo_ref, held = refs[2 * lines :]
    r, z, h = place[0], place[1], place[2]
    n, width = pieces[0].shape[1:]
    step = math.gcd(n, rb)
    for d in range(lines):
        line = r ^ d
        for which in range(2):
            core = h if which == 0 else 1 - h
            for m in range(lines):
                plane = (z + lines - m) % lines
                for i in range(n // step):
                    flat = line * n + i * step
                    row = (flat // rb) * width + (plane * 2 + core) * rb + flat % rb
                    row = pl.multiple_of(row, 8)
                    held[pl.ds(row, step), :] = pieces[2 * d + which][m, i * step : (i + 1) * step, :]
    panels, depth, _ = hi_ref.shape

    @pl.loop(0, panels * depth // width)
    def _(i):
        row = pl.multiple_of(i * width, width)
        value = held[pl.ds(row, width), :]
        hi = value.astype(jnp.bfloat16)
        p = row // depth
        at = pl.multiple_of(row % depth, width)
        hi_ref[p, pl.ds(at, width), :] = hi
        lo_ref[p, pl.ds(at, width), :] = (value - hi.astype(jnp.float32)).astype(jnp.bfloat16)


def product_kernel(panel_ids, slots, rb, lo, hi, info, where, g_ref, *refs):
    count = len(panel_ids)
    x_hi, x_lo = refs[:count], refs[count : 2 * count]
    mine, other = refs[2 * count :]
    side, tile = pl.program_id(0), pl.program_id(1)
    tile_slots, rows, depth = g_ref.shape
    h = info[4]

    @pl.when(info[2 + side] > 0)
    def _():
        g = g_ref[...].reshape(tile_slots * rows, depth)
        g_hi = g.astype(jnp.bfloat16)
        g_lo = (g - g_hi.astype(jnp.float32)).astype(jnp.bfloat16)
        dot = functools.partial(jnp.dot, preferred_element_type=jnp.float32)
        for k, p in enumerate(panel_ids):
            value = dot(g_hi, x_hi[k][0]) + (dot(g_hi, x_lo[k][0]) + dot(g_lo, x_hi[k][0]))
            for s in range(tile_slots):
                at = where[p * slots + tile * tile_slots + s]
                top = value[s * rows : s * rows + rb]
                bottom = value[s * rows + rb : (s + 1) * rows]

                @pl.when((at >= lo) & (at < hi))
                def _(at=at, top=top, bottom=bottom):
                    mine[side, at - lo] = jnp.where(h == 0, top, bottom)
                    other[side, at - lo] = jnp.where(h == 0, bottom, top)


def product(g3, xs, panel_ids, lo, hi, rb, info, where, sides):
    slots, width, depth = g3.shape
    columns = xs[0][0].shape[2]
    rows = 2 * rb
    tile_slots = math.gcd(slots, max(1, 256 // rows))
    grid = (sides, slots // tile_slots)

    def g_map(side, tile, info, where):
        return (jnp.where(info[2 + side] > 0, tile, 0), info[side], 0)

    x_specs = [
        pl.BlockSpec((1, depth, columns), functools.partial(lambda at, a, b, i, w: (at, 0, 0), at))
        for _, _, at in xs
    ]
    out = jax.ShapeDtypeStruct((sides, hi - lo, rb, columns), jnp.float32)
    out_spec = pl.BlockSpec(out.shape, lambda a, b, i, w: (0, 0, 0, 0))
    flops = 6 * slots * rows * depth * columns * len(xs)
    return pl.pallas_call(
        functools.partial(product_kernel, panel_ids, slots, rb, lo, hi),
        out_shape=(out, out),
        grid_spec=pltpu.PrefetchScalarGridSpec(
            num_scalar_prefetch=2,
            grid=grid,
            in_specs=[pl.BlockSpec((tile_slots, rows, depth), g_map)] + x_specs + x_specs,
            out_specs=(out_spec, out_spec),
        ),
        compiler_params=pltpu.CompilerParams(vmem_limit_bytes=VMEM_LIMIT),
        cost_estimate=pl.CostEstimate(
            flops=flops, bytes_accessed=slots * rows * depth * 4, transcendentals=0
        ),
    )(info, where, g3, *[x[0] for x in xs], *[x[1] for x in xs])


def finish_kernel(parts, bounds, where, n_ref, *refs):
    ins = refs[: 4 * parts]
    panel_ref, diag_ref, total = refs[4 * parts :]
    panels, slots, rb, width = n_ref.shape
    for k in range(parts):
        own, swapped, up, down = ins[4 * k : 4 * k + 4]
        total[bounds[k] : bounds[k + 1]] = (own[0] + swapped[0]) + (up[...] + down[...])
    for p in range(panels):
        for s in range(slots):
            at = where[p * slots + s]
            value = total[jnp.maximum(at, 0)]
            panel_ref[p, s] = jnp.where(at >= 0, -value, 0.0)
        diag_ref[p] = lax.dot_general(
            n_ref[p].reshape(slots * rb, width),
            panel_ref[p].reshape(slots * rb, width),
            (((0,), (0,)), ((), ())),
            precision=HIGHEST,
            preferred_element_type=jnp.float32,
        )


def on_device(
    lines, inverse_matrix, factor_blocks, factor_inverse, diag_given, block_lists, list_mask, slot_of_block
):
    panels, slots, rb, width = factor_blocks.shape
    halves = inverse_matrix.shape[1] // width
    f32 = jnp.float32
    r = lax.axis_index("prow").astype(jnp.int32)
    col = lax.axis_index("pcol").astype(jnp.int32)
    z, h = col // 2, col % 2
    place = jnp.stack([r, z, h])

    def send(value, to):
        pairs = []
        for a in range(lines):
            for b in range(lines):
                for c in range(2):
                    target = to(a, b, c)
                    if target is not None:
                        ta, tb, tc = target
                        pairs.append(((a * lines + b) * 2 + c, (ta * lines + tb) * 2 + tc))
        return lax.ppermute(value, AXES, pairs)

    def swap(value):
        return send(value, lambda a, b, c: (a, b, 1 - c))

    def across(value, d):
        return send(value, lambda a, b, c: (a ^ d, b, c))

    def along(value, m):
        return send(value, lambda a, b, c: (a, (b + m) % lines, c))

    slot_valid = valid_slots(block_lists, list_mask, slot_of_block)
    row_valid = lax.dynamic_slice_in_dim(slot_valid, r * slots, slots, 1).reshape(panels * slots)
    order = jnp.arange(panels * slots, dtype=jnp.int32)
    before = jnp.sum(jnp.where(order[None, :] < order[:, None], row_valid[None, :], 0), axis=1)
    where = jnp.where(row_valid > 0, before, -1).astype(jnp.int32)

    keep = 3 * panels * slots // 4
    half = panels // 2
    groups = [tuple(range(half)), tuple(range(half, panels))]
    first = keep - slots * (panels - half)
    bounds = [0, first, keep]
    chunk_panels = [tuple(range(half)), tuple(range(half - 1, panels))]

    part_shapes = [(2, len(g) * halves * rb // lines, width) for g in groups]
    made = call(
        functools.partial(normalize_kernel, groups, lines),
        [jax.ShapeDtypeStruct(factor_blocks.shape, f32)]
        + [jax.ShapeDtypeStruct(s, f32) for s in part_shapes for _ in range(lines)],
        [pltpu.VMEM((2, len(g) * halves * rb, width), f32) for g in groups],
        n_scalar=2, n_in=2, flops=12 * factor_blocks.size * width, moved=12 * factor_blocks.size,
    )(place, row_valid, factor_blocks, factor_inverse)
    normalized = made[0]

    split = []
    for g, group in enumerate(groups):
        parts = made[1 + g * lines : 1 + (g + 1) * lines]
        shape = part_shapes[g]
        moved = 8 * lines * math.prod(shape)
        held = [parts[0]] + [across(parts[d], d) for d in range(1, lines)]
        outgoing = call(
            functools.partial(to_planes_kernel, lines),
            [jax.ShapeDtypeStruct(shape, f32)] * lines, n_in=lines, moved=moved,
        )(place, *held)
        held = [outgoing[0]] + [along(outgoing[m], m) for m in range(1, lines)]
        piece = jax.ShapeDtypeStruct((lines,) + shape[1:], f32)
        mine, other = call(
            functools.partial(by_core_kernel, lines), [piece, piece], n_in=lines, moved=moved
        )(place, *held)
        swapped = swap(other)
        pieces = [mine, swapped]
        if lines == 4:
            mine_1, swapped_1 = across(mine, 1), across(swapped, 1)
            mine_2, swapped_2 = across(mine, 2), across(swapped, 2)
            pieces += [mine_1, swapped_1, mine_2, swapped_2]
            pieces += [across(mine_1, 2), across(swapped_2, 1)]
        else:
            for d in range(1, lines):
                pieces += [across(mine, d), across(swapped, d)]
        block = jax.ShapeDtypeStruct((len(group), halves * width, width), jnp.bfloat16)
        x_hi, x_lo = call(
            functools.partial(assemble_kernel, lines, rb),
            [block, block],
            [pltpu.VMEM((len(group) * halves * width, width), f32)],
            n_in=2 * lines, moved=8 * len(group) * halves * width * width,
        )(place, *pieces)
        split += [(x_hi, x_lo, at) for at in range(len(group))]

    g3 = inverse_matrix.reshape(slots, width, halves * width)
    flag = lambda value: value.astype(jnp.int32)
    finals = []
    for k, ids in enumerate(chunk_panels):
        lo, hi = bounds[k], bounds[k + 1]
        xs = [split[p] for p in ids]
        make = functools.partial(product, g3, xs, ids, lo, hi, rb)
        up = down = None
        for step in range(lines - 1):
            j_up = lines - 1 - step + z
            j_down = step - (lines - 1 - z)
            info = jnp.stack([
                jnp.clip(j_up, 0, lines - 1), jnp.clip(j_down, 0, lines - 1),
                flag(z <= step), flag(z >= lines - 1 - step), h,
            ])
            mine, other = make(info, where, 2)
            swapped = swap(other)
            send_up = mine[0] + swapped[0]
            send_down = mine[1] + swapped[1]
            if step:
                send_up = send_up + up
                send_down = send_down + down
            up = send(send_up, lambda a, b, c: (a, b + 1, c) if b <= step else None)
            down = send(send_down, lambda a, b, c: (a, b - 1, c) if b >= lines - 1 - step else None)
        info = jnp.stack([z, z, jnp.int32(1), jnp.int32(1), h])
        own, other = make(info, where, 1)
        finals += [own, swap(other), up, down]

    panel_inverse, terms = call(
        functools.partial(finish_kernel, len(chunk_panels), bounds),
        [
            jax.ShapeDtypeStruct(factor_blocks.shape, f32),
            jax.ShapeDtypeStruct(factor_inverse.shape, f32),
        ],
        [pltpu.VMEM((keep, rb, width), f32)],
        n_in=1 + len(finals), flops=12 * factor_blocks.size * width, moved=20 * factor_blocks.size,
    )(where, normalized, *finals)

    pick = lambda value, at: lax.dynamic_index_in_dim(value, at, 0, False)
    two = terms.reshape(2, half * width, width)
    total = pick(two, h) + swap(pick(two, 1 - h))
    parts = total.reshape(lines, -1, width)
    total = pick(parts, r)
    for piece in [across(pick(parts, r ^ d), d) for d in range(1, lines)]:
        total = total + piece
    parts = total.reshape(lines, -1, width)
    total = pick(parts, z)
    for piece in [along(pick(parts, (z + m) % lines), m) for m in range(1, lines)]:
        total = total + piece
    pieces = [total] + [along(total, m) for m in range(1, lines)]
    gathered = jnp.zeros((lines,) + total.shape, f32)
    for m in range(lines):
        gathered = lax.dynamic_update_index_in_dim(gathered, pieces[m], (z - m) % lines, 0)
    total = gathered.reshape(-1, width)
    pieces = [total] + [across(total, d) for d in range(1, lines)]
    gathered = jnp.zeros((lines,) + total.shape, f32)
    for d in range(lines):
        gathered = lax.dynamic_update_index_in_dim(gathered, pieces[d], r ^ d, 0)
    total = gathered.reshape(half, width, width)
    swapped = swap(total)
    summed = jnp.concatenate([jnp.where(h == 0, total, swapped), jnp.where(h == 0, swapped, total)], 0)
    return (panel_inverse, diag_given - summed)


def solution(mesh):
    lines = mesh.shape["prow"]
    if mesh.shape["pcol"] != 2 * lines:
        raise ValueError("mesh shape")
    placed = (P("prow", "pcol"), P(None, "prow", "pcol", None), P(), P(), P(), P(), P())
    return jax.shard_map(
        functools.partial(on_device, lines),
        mesh=mesh,
        in_specs=placed,
        out_specs=(P(None, "prow", "pcol", None), P()),
        check_vma=False,
    )
```

```python
import functools
import math
import jax
import jax.numpy as jnp
from jax import lax
from jax.experimental import pallas as pl
from jax.experimental.pallas import tpu as pltpu
from jax.sharding import PartitionSpec as P

AXES = ("prow", "pcol")
HIGHEST = lax.Precision.HIGHEST
VMEM_LIMIT = 56 * 1024 * 1024


def whole(memory_space=pltpu.VMEM):
    return pl.BlockSpec(memory_space=memory_space)


def call(kernel, outs, scratch=(), n_scalar=1, n_in=1, n_after=0, flops=0, moved=0):
    used = n_scalar + n_in

    def body(*refs):
        kernel(*refs[:used], *refs[used + n_after :])

    return pl.pallas_call(
        body,
        out_shape=outs,
        in_specs=[whole(pltpu.SMEM)] * n_scalar + [whole()] * n_in + [whole(pl.ANY)] * n_after,
        out_specs=jax.tree.map(lambda _: whole(), outs),
        scratch_shapes=list(scratch),
        compiler_params=pltpu.CompilerParams(vmem_limit_bytes=VMEM_LIMIT),
        cost_estimate=pl.CostEstimate(flops=flops, bytes_accessed=moved, transcendentals=0),
    )


def valid_slots(block_lists, list_mask, slot_of_block):
    window_blocks = block_lists.shape[1]
    block_ids = jnp.arange(window_blocks, dtype=jnp.int32)
    chosen = (block_lists[:, :, None] == block_ids[None, None, :]).astype(jnp.int32)
    slot_ids = jnp.sum(chosen * slot_of_block[None, None, :], axis=2)
    matches = (slot_ids[:, :, None] == block_ids[None, None, :]).astype(jnp.int32)
    return jnp.sum(matches * list_mask[:, :, None], axis=1)


def normalize_kernel(group, lines, place, valid, f_ref, partner_ref, inv_ref, n_ref, *rest):
    slots, rb, width = f_ref.shape[1:]
    halves = slots // 2
    outs, scratch = rest[:lines], rest[lines]
    r, h = place[0], place[2]
    rows = halves * rb

    def times(block, p):
        return jnp.dot(block, inv_ref[p], precision=HIGHEST, preferred_element_type=jnp.float32)

    for at, p in enumerate(group):
        block = times(f_ref[p].reshape(slots * rb, width), p)
        for s in range(slots):
            one = block[s * rb : (s + 1) * rb]
            n_ref[at, s] = jnp.where(valid[p * slots + s] > 0, one, 0.0)
        block = times(partner_ref[p].reshape(rows, width), p)
        for t in range(halves):
            one = block[t * rb : (t + 1) * rb]
            row = at * rows + t * rb
            used = valid[p * slots + h * halves + t] > 0
            scratch[1 - h, row : row + rb] = jnp.where(used, one, 0.0)
            scratch[h, row : row + rb] = n_ref[at, h * halves + t]
    n = len(group) * rows // lines
    for d in range(lines):
        start = pl.multiple_of((r ^ d) * n, 8)
        outs[d][...] = scratch[:, pl.ds(start, n), :]


def to_planes_kernel(lines, place, *refs):
    r, z = place[0], place[1]
    for m in range(lines):
        which = r ^ ((z + m) % lines)
        for d in range(lines):

            @pl.when(which == d)
            def _(m=m, d=d):
                refs[lines + m][...] = refs[d][...]


def stack_kernel(place, *refs):
    for m in range(len(refs) - 1):
        refs[-1][:, m] = refs[m][...]


def assemble_kernel(lines, rb, place, *refs):
    pieces, (hi_ref, lo_ref, held) = refs[:-3], refs[-3:]
    r, z = place[0], place[1]
    n, width = pieces[0].shape[2:]
    step = math.gcd(n, rb)
    for d in range(lines):
        line = r ^ d
        for core in range(2):
            if len(pieces) > lines and d == lines - 1:
                piece, at = pieces[d + core], 0
            else:
                piece, at = pieces[d], core
            for m in range(lines):
                plane = (z + lines - m) % lines
                for i in range(n // step):
                    flat = line * n + i * step
                    row = (flat // rb) * width + (plane * 2 + core) * rb + flat % rb
                    row = pl.multiple_of(row, 8)
                    held[pl.ds(row, step), :] = piece[at, m, i * step : (i + 1) * step, :]
    panels, depth, _ = hi_ref.shape

    @pl.loop(0, panels * depth // width)
    def _(i):
        row = pl.multiple_of(i * width, width)
        value = held[pl.ds(row, width), :]
        hi = value.astype(jnp.bfloat16)
        p = row // depth
        at = pl.multiple_of(row % depth, width)
        hi_ref[p, pl.ds(at, width), :] = hi
        lo_ref[p, pl.ds(at, width), :] = (value - hi.astype(jnp.float32)).astype(jnp.bfloat16)


def product_kernel(panel_ids, slots, rb, lo, hi, waits, info, where, g_ref, *refs):
    count = len(panel_ids)
    x_hi, x_lo = refs[:count], refs[count : 2 * count]
    mine, other, held, done = refs[2 * count + waits :]
    tile = pl.program_id(0)
    tile_slots, rows, depth = g_ref.shape
    size = hi - lo
    h = info[1]
    g = g_ref[...].reshape(tile_slots * rows, depth)
    g_hi = g.astype(jnp.bfloat16)
    g_lo = (g - g_hi.astype(jnp.float32)).astype(jnp.bfloat16)
    dot = functools.partial(jnp.dot, preferred_element_type=jnp.float32)
    for k, p in enumerate(panel_ids):
        value = dot(g_hi, x_hi[k][0]) + (dot(g_hi, x_lo[k][0]) + dot(g_lo, x_hi[k][0]))
        for s in range(tile_slots):
            at = where[p * slots + tile * tile_slots + s]
            at = jnp.where((at >= lo) & (at < hi), at - lo, size)
            for core in range(2):
                start = s * rows + core * rb
                held[(core + h) % 2, at] = value[start : start + rb]

    @pl.when(tile == pl.num_programs(0) - 1)
    def _():
        first = pltpu.make_async_copy(held.at[0, pl.ds(0, size)], mine, done.at[0])
        second = pltpu.make_async_copy(held.at[1, pl.ds(0, size)], other, done.at[1])
        first.start()
        second.start()
        first.wait()
        second.wait()


def product(g3, xs, panel_ids, lo, hi, rb, info, where, after):
    slots, width, depth = g3.shape
    columns = xs[0][0].shape[2]
    rows = 2 * rb
    tile_slots = math.gcd(slots, max(1, 256 // rows))
    x_specs = [
        pl.BlockSpec((1, depth, columns), functools.partial(lambda at, a, i, w: (at, 0, 0), at))
        for _, _, at in xs
    ]
    out = jax.ShapeDtypeStruct((hi - lo, rb, columns), jnp.float32)
    anywhere = pl.BlockSpec(memory_space=pl.ANY)
    return pl.pallas_call(
        functools.partial(product_kernel, panel_ids, slots, rb, lo, hi, len(after)),
        out_shape=(out, out),
        grid_spec=pltpu.PrefetchScalarGridSpec(
            num_scalar_prefetch=2,
            grid=(slots // tile_slots,),
            in_specs=[pl.BlockSpec((tile_slots, rows, depth), lambda tile, i, w: (tile, i[0], 0))]
            + x_specs + x_specs + [anywhere] * len(after),
            out_specs=(anywhere, anywhere),
            scratch_shapes=[
                pltpu.VMEM((2, hi - lo + 1, rb, columns), jnp.float32),
                pltpu.SemaphoreType.DMA((2,)),
            ],
        ),
        compiler_params=pltpu.CompilerParams(vmem_limit_bytes=VMEM_LIMIT),
        cost_estimate=pl.CostEstimate(
            flops=12 * slots * rows * depth * columns * len(xs),
            bytes_accessed=slots * rows * depth * 4, transcendentals=0,
        ),
    )(info, where, g3, *[x[0] for x in xs], *[x[1] for x in xs], *after)


def finish_kernel(parts, bounds, groups, where, *refs):
    n_refs, refs = refs[: len(groups)], refs[len(groups) :]
    ins = refs[: 4 * parts]
    panel_ref, diag_ref, total = refs[4 * parts :]
    panels, slots, rb, width = panel_ref.shape
    n_of = {p: n_refs[g][at] for g, group in enumerate(groups) for at, p in enumerate(group)}
    for k in range(parts):
        own, swapped, up, down = ins[4 * k : 4 * k + 4]
        total[bounds[k] : bounds[k + 1]] = (own[...] + swapped[...]) + (up[...] + down[...])
    for p in range(panels):
        for s in range(slots):
            at = where[p * slots + s]
            value = total[jnp.maximum(at, 0)]
            panel_ref[p, s] = jnp.where(at >= 0, -value, 0.0)
        diag_ref[p] = lax.dot_general(
            n_of[p].reshape(slots * rb, width),
            panel_ref[p].reshape(slots * rb, width),
            (((0,), (0,)), ((), ())),
            precision=HIGHEST,
            preferred_element_type=jnp.float32,
        )


def on_device(
    lines, inverse_matrix, factor_blocks, factor_inverse, diag_given, block_lists, list_mask, slot_of_block
):
    panels, slots, rb, width = factor_blocks.shape
    halves = inverse_matrix.shape[1] // width
    f32 = jnp.float32
    r = lax.axis_index("prow").astype(jnp.int32)
    col = lax.axis_index("pcol").astype(jnp.int32)
    z, h = col // 2, col % 2
    place = jnp.stack([r, z, h])

    def send(value, to):
        pairs = []
        for a in range(lines):
            for b in range(lines):
                for c in range(2):
                    target = to(a, b, c)
                    if target is not None:
                        ta, tb, tc = target
                        pairs.append(((a * lines + b) * 2 + c, (ta * lines + tb) * 2 + tc))
        return lax.ppermute(value, AXES, pairs)

    def swap(value):
        return send(value, lambda a, b, c: (a, b, 1 - c))

    def across(value, d):
        return send(value, lambda a, b, c: (a ^ d, b, c))

    def along(value, m):
        return send(value, lambda a, b, c: (a, (b + m) % lines, c))

    slot_valid = valid_slots(block_lists, list_mask, slot_of_block)
    row_valid = lax.dynamic_slice_in_dim(slot_valid, r * slots, slots, 1).reshape(panels * slots)
    order = jnp.arange(panels * slots, dtype=jnp.int32)
    before = jnp.sum(jnp.where(order[None, :] < order[:, None], row_valid[None, :], 0), axis=1)
    where = jnp.where(row_valid > 0, before, -1).astype(jnp.int32)

    keep = 3 * panels * slots // 4
    half = panels // 2
    groups = [tuple(range(half)), tuple(range(half, panels))]
    ends = [g[-1] + 1 for g in groups]
    bounds = [0] + [keep - slots * (panels - end) for end in ends]
    chunk_panels = [tuple(range(lo // slots, end)) for lo, end in zip(bounds, ends)]

    split, normalized, parts_of, planes, stacked, gathered = [], [], [], [], [], []

    def normalize(group, after):
        shape = (2, len(group) * halves * rb // lines, width)
        rows_made = jax.ShapeDtypeStruct((len(group), slots, rb, width), f32)
        made = call(
            functools.partial(normalize_kernel, group, lines),
            [rows_made] + [jax.ShapeDtypeStruct(shape, f32)] * lines,
            [pltpu.VMEM((2, len(group) * halves * rb, width), f32)],
            n_scalar=2, n_in=3, n_after=len(after),
            flops=6 * lines * math.prod(shape) * width, moved=8 * lines * math.prod(shape),
        )(place, row_valid, factor_blocks, partner, factor_inverse, *after)
        normalized.append(made[0])
        parts_of.append(made[1:])

    partner = swap(lax.dynamic_slice_in_dim(factor_blocks, (1 - h) * halves, halves, 1))
    spread = []
    gather_after = []
    for g, group in enumerate(groups):
        normalize(group, spread)
        parts = parts_of[g]
        moved = 8 * lines * math.prod(parts[0].shape)
        held = [parts[0]] + [across(parts[d], d) for d in range(1, lines)]
        outgoing = call(
            functools.partial(to_planes_kernel, lines),
            [jax.ShapeDtypeStruct(parts[0].shape, f32)] * lines, n_in=lines, moved=moved,
        )(place, *held)
        spread = [outgoing[0]]
        planes.append(outgoing)
    for g, group in enumerate(groups):
        outgoing = planes[g]
        shape = outgoing[0].shape
        held = [outgoing[0]] + [along(outgoing[m], m) for m in range(1, lines)]
        after = gather_after + ([planes[g + 1][0]] if g + 1 < len(groups) else [])
        [both] = call(
            stack_kernel, [jax.ShapeDtypeStruct((2, lines) + shape[1:], f32)], n_in=lines,
            n_after=len(after), moved=8 * lines * math.prod(shape),
        )(place, *held, *after)
        pieces = [both] + [across(both, d) for d in range(1, lines)]
        if lines == 4:
            pieces[3:] = [across(pieces[1][:1], 2), across(pieces[2][1:], 1)]
        gather_after = pieces[-2:]
        stacked.append(both)
        gathered.append(pieces)
    for g, group in enumerate(groups):
        pieces, after = gathered[g], stacked[g + 1 : g + 2]
        block = jax.ShapeDtypeStruct((len(group), halves * width, width), jnp.bfloat16)
        x_hi, x_lo = call(
            functools.partial(assemble_kernel, lines, rb),
            [block, block],
            [pltpu.VMEM((len(group) * halves * width, width), f32)],
            n_in=len(pieces), n_after=len(after), moved=8 * len(group) * halves * width * width,
        )(place, *pieces, *after)
        split += [(x_hi, x_lo, at) for at in range(len(group))]

    g3 = inverse_matrix.reshape(slots, width, halves * width)
    order = [
        sorted(
            (j for j in range(lines) if j != a),
            key=lambda j: (lines - 1 - j + a, 0) if j > a else (j + lines - 1 - a, 1),
        )
        + [a]
        for a in range(lines)
    ]

    def of_plane(values):
        return sum(jnp.where(z == a, jnp.int32(v), 0) for a, v in enumerate(values))

    def chosen(made, calls):
        kinds = sorted({c for c in calls if c is not None})
        value = made[kinds[-1]][0] + made[kinds[-1]][1]
        for c in kinds[:-1]:
            here = functools.reduce(jnp.logical_or, [z == a for a in range(lines) if calls[a] == c])
            value = jnp.where(here, made[c][0] + made[c][1], value)
        return value

    finals, after, arrived = [], [], []
    for k, ids in enumerate(chunk_panels):
        lo, hi = bounds[k], bounds[k + 1]
        xs = [split[p] for p in ids]
        made = []

        def compute(after):
            n = len(made)
            info = jnp.stack([of_plane([order[a][n] for a in range(lines)]), h])
            mine, other = product(g3, xs, ids, lo, hi, rb, info, where, after)
            made.append((mine, swap(other)))
            return [mine]

        compute(after)
        up = down = None
        for step in range(lines - 1):
            rises = [order[a].index(lines - 1 - step + a) if a <= step else None for a in range(lines)]
            sinks = [order[a].index(step - lines + 1 + a) if a >= lines - 1 - step else None for a in range(lines)]
            send_up, send_down = chosen(made, rises), chosen(made, sinks)
            if step:
                send_up, send_down = send_up + up, send_down + down
            up = send(send_up, lambda a, b, c: (a, b + 1, c) if b <= step else None)
            down = send(send_down, lambda a, b, c: (a, b - 1, c) if b >= lines - 1 - step else None)
            if step == 0:
                after = [send_up, send_down]
                for n in range(lines - 2):
                    after = compute(after + (arrived if n == 0 else []))
            elif step == 1:
                compute([send_up, send_down])
        after = [send_up, send_down, made[lines - 1][0]]
        arrived = [up, down]
        finals += [*made[lines - 1], up, down]

    panel_inverse, terms = call(
        functools.partial(finish_kernel, len(chunk_panels), bounds, groups),
        [
            jax.ShapeDtypeStruct(factor_blocks.shape, f32),
            jax.ShapeDtypeStruct(factor_inverse.shape, f32),
        ],
        [pltpu.VMEM((keep, rb, width), f32)],
        n_in=len(groups) + len(finals), flops=12 * factor_blocks.size * width, moved=20 * factor_blocks.size,
    )(where, *normalized, *finals)

    pick = lambda value, at: lax.dynamic_index_in_dim(value, at, 0, False)
    two = terms.reshape(2, half * width, width)
    total = pick(two, h) + swap(pick(two, 1 - h))
    parts = total.reshape(lines, -1, width)
    total = pick(parts, r)
    for piece in [across(pick(parts, r ^ d), d) for d in range(1, lines)]:
        total = total + piece
    parts = total.reshape(lines, -1, width)
    total = pick(parts, z)
    for piece in [along(pick(parts, (z + m) % lines), m) for m in range(1, lines)]:
        total = total + piece
    pieces = [total] + [along(total, m) for m in range(1, lines)]
    gathered = jnp.zeros((lines,) + total.shape, f32)
    for m in range(lines):
        gathered = lax.dynamic_update_index_in_dim(gathered, pieces[m], (z - m) % lines, 0)
    total = gathered.reshape(-1, width)
    pieces = [total] + [across(total, d) for d in range(1, lines)]
    gathered = jnp.zeros((lines,) + total.shape, f32)
    for d in range(lines):
        gathered = lax.dynamic_update_index_in_dim(gathered, pieces[d], r ^ d, 0)
    total = gathered.reshape(half, width, width)
    swapped = swap(total)
    summed = jnp.concatenate([jnp.where(h == 0, total, swapped), jnp.where(h == 0, swapped, total)], 0)
    return (panel_inverse, diag_given - summed)


def solution(mesh):
    lines = mesh.shape["prow"]
    if mesh.shape["pcol"] != 2 * lines:
        raise ValueError("mesh shape")
    placed = (P("prow", "pcol"), P(None, "prow", "pcol", None), P(), P(), P(), P(), P())
    return jax.shard_map(
        functools.partial(on_device, lines),
        mesh=mesh,
        in_specs=placed,
        out_specs=(P(None, "prow", "pcol", None), P()),
        check_vma=False,
    )
```

```python
import functools
import math
import jax
import jax.numpy as jnp
from jax import lax
from jax.experimental import pallas as pl
from jax.experimental.pallas import tpu as pltpu
from jax.sharding import PartitionSpec as P

AXES = ("prow", "pcol")
HIGHEST = lax.Precision.HIGHEST
VMEM_LIMIT = 56 * 1024 * 1024


def whole(memory_space=pltpu.VMEM):
    return pl.BlockSpec(memory_space=memory_space)


def call(kernel, outs, scratch=(), n_scalar=1, n_in=1, n_after=0, flops=0, moved=0):
    used = n_scalar + n_in

    def body(*refs):
        kernel(*refs[:used], *refs[used + n_after :])

    return pl.pallas_call(
        body,
        out_shape=outs,
        in_specs=[whole(pltpu.SMEM)] * n_scalar + [whole()] * n_in + [whole(pl.ANY)] * n_after,
        out_specs=jax.tree.map(lambda _: whole(), outs),
        scratch_shapes=list(scratch),
        compiler_params=pltpu.CompilerParams(vmem_limit_bytes=VMEM_LIMIT),
        cost_estimate=pl.CostEstimate(flops=flops, bytes_accessed=moved, transcendentals=0),
    )


def valid_slots(block_lists, list_mask, slot_of_block):
    window_blocks = block_lists.shape[1]
    block_ids = jnp.arange(window_blocks, dtype=jnp.int32)
    chosen = (block_lists[:, :, None] == block_ids[None, None, :]).astype(jnp.int32)
    slot_ids = jnp.sum(chosen * slot_of_block[None, None, :], axis=2)
    matches = (slot_ids[:, :, None] == block_ids[None, None, :]).astype(jnp.int32)
    return jnp.sum(matches * list_mask[:, :, None], axis=1)


def normalize_kernel(group, lines, place, valid, f_ref, partner_ref, inv_ref, n_ref, *rest):
    slots, rb, width = f_ref.shape[1:]
    halves = slots // 2
    outs, scratch = rest[:lines], rest[lines]
    r, h = place[0], place[2]
    rows = halves * rb

    def times(block, p):
        return jnp.dot(block, inv_ref[p], precision=HIGHEST, preferred_element_type=jnp.float32)

    for at, p in enumerate(group):
        block = times(f_ref[p].reshape(slots * rb, width), p)
        for s in range(slots):
            one = block[s * rb : (s + 1) * rb]
            n_ref[at, s] = jnp.where(valid[p * slots + s] > 0, one, 0.0)
        block = times(partner_ref[p].reshape(rows, width), p)
        for t in range(halves):
            one = block[t * rb : (t + 1) * rb]
            row = at * rows + t * rb
            used = valid[p * slots + h * halves + t] > 0
            scratch[1 - h, row : row + rb] = jnp.where(used, one, 0.0)
            scratch[h, row : row + rb] = n_ref[at, h * halves + t]
    n = len(group) * rows // lines
    for d in range(lines):
        start = pl.multiple_of((r ^ d) * n, 8)
        outs[d][...] = scratch[:, pl.ds(start, n), :]


def to_planes_kernel(lines, place, *refs):
    r, z = place[0], place[1]
    for m in range(lines):
        which = r ^ ((z + m) % lines)
        for d in range(lines):

            @pl.when(which == d)
            def _(m=m, d=d):
                refs[lines + m][...] = refs[d][...]


def stack_kernel(place, *refs):
    for m in range(len(refs) - 1):
        refs[-1][:, m] = refs[m][...]


def halves_kernel(first_ref, second_ref, first_half, second_half):
    first_half[...] = first_ref[:1]
    second_half[...] = second_ref[1:]


def assemble_kernel(lines, rb, place, *refs):
    pieces, (hi_ref, lo_ref, held) = refs[:-3], refs[-3:]
    r, z = place[0], place[1]
    n, width = pieces[0].shape[2:]
    step = math.gcd(n, rb)
    for d in range(lines):
        line = r ^ d
        for core in range(2):
            if len(pieces) > lines and d == lines - 1:
                piece, at = pieces[d + core], 0
            else:
                piece, at = pieces[d], core
            for m in range(lines):
                plane = (z + lines - m) % lines
                for i in range(n // step):
                    flat = line * n + i * step
                    row = (flat // rb) * width + (plane * 2 + core) * rb + flat % rb
                    row = pl.multiple_of(row, 8)
                    held[pl.ds(row, step), :] = piece[at, m, i * step : (i + 1) * step, :]
    panels, depth, _ = hi_ref.shape

    @pl.loop(0, panels * depth // width)
    def _(i):
        row = pl.multiple_of(i * width, width)
        value = held[pl.ds(row, width), :]
        hi = value.astype(jnp.bfloat16)
        p = row // depth
        at = pl.multiple_of(row % depth, width)
        hi_ref[p, pl.ds(at, width), :] = hi
        lo_ref[p, pl.ds(at, width), :] = (value - hi.astype(jnp.float32)).astype(jnp.bfloat16)


def product_kernel(panels, slots, bounds, waits, info, where, g_ref, *refs):
    x_hi, x_lo = refs[:panels], refs[panels : 2 * panels]
    outs, held, done = refs[2 * panels + waits : -2], refs[-2], refs[-1]
    tile = pl.program_id(0)
    tile_slots, rows, depth = g_ref.shape
    g = g_ref[...].reshape(tile_slots * rows, depth)
    g_hi = g.astype(jnp.bfloat16)
    g_lo = (g - g_hi.astype(jnp.float32)).astype(jnp.bfloat16)
    dot = functools.partial(jnp.dot, preferred_element_type=jnp.float32)
    for p in range(panels):
        value = dot(g_hi, x_hi[p][0]) + (dot(g_hi, x_lo[p][0]) + dot(g_lo, x_hi[p][0]))
        for s in range(tile_slots):
            at = where[p * slots + tile * tile_slots + s]
            held[jnp.where(at >= 0, at, bounds[-1])] = value[s * rows : (s + 1) * rows]

    @pl.when(tile == pl.num_programs(0) - 1)
    def _():
        copies = [
            pltpu.make_async_copy(held.at[pl.ds(bounds[k], bounds[k + 1] - bounds[k])], out, done.at[k])
            for k, out in enumerate(outs)
        ]
        for copy in copies:
            copy.start()
        for copy in copies:
            copy.wait()


def product(g3, xs, bounds, rb, info, where, after):
    slots, width, depth = g3.shape
    columns = xs[0][0].shape[2]
    rows = 2 * rb
    tile_slots = math.gcd(slots, max(1, 256 // rows))
    x_specs = [
        pl.BlockSpec((1, depth, columns), functools.partial(lambda at, a, i, w: (at, 0, 0), at))
        for _, _, at in xs
    ]
    anywhere = pl.BlockSpec(memory_space=pl.ANY)
    pieces = len(bounds) - 1
    return pl.pallas_call(
        functools.partial(product_kernel, len(xs), slots, bounds, len(after)),
        out_shape=[
            jax.ShapeDtypeStruct((bounds[k + 1] - bounds[k], rows, columns), jnp.float32) for k in range(pieces)
        ],
        grid_spec=pltpu.PrefetchScalarGridSpec(
            num_scalar_prefetch=2,
            grid=(slots // tile_slots,),
            in_specs=[pl.BlockSpec((tile_slots, rows, depth), lambda tile, i, w: (tile, i[0], 0))]
            + x_specs + x_specs + [anywhere] * len(after),
            out_specs=[anywhere] * pieces,
            scratch_shapes=[
                pltpu.VMEM((bounds[-1] + 1, rows, columns), jnp.float32),
                pltpu.SemaphoreType.DMA((pieces,)),
            ],
        ),
        compiler_params=pltpu.CompilerParams(vmem_limit_bytes=VMEM_LIMIT),
        cost_estimate=pl.CostEstimate(
            flops=12 * slots * rows * depth * columns * len(xs),
            bytes_accessed=slots * rows * depth * 4, transcendentals=0,
        ),
    )(info, where, g3, *[x[0] for x in xs], *[x[1] for x in xs], *after)


def merge_kernel(bounds, lines, place, *refs):
    mine, other = refs[-2:]
    rb = mine.shape[1]
    from_others = place[1] != jnp.where(place[2] == 0, 0, lines - 1)
    for core in range(2):
        rows = slice(core * rb, (core + 1) * rb)

        def fill(out, rows=rows):
            for k in range(len(bounds) - 1):
                arrived = jnp.where(from_others, refs[2 * k + 1][:, rows, :], 0.0)
                value = refs[2 * k][:, rows, :] + arrived
                out[bounds[k] : bounds[k + 1]] = value

        pl.when(place[2] == core)(functools.partial(fill, mine))
        pl.when(place[2] != core)(functools.partial(fill, other))


def finish_kernel(groups, where, *refs):
    n_refs, refs = refs[: len(groups)], refs[len(groups) :]
    mine, swapped, panel_ref, diag_ref, total = refs
    total[...] = mine[...] + swapped[...]
    panels, slots, rb, width = panel_ref.shape
    n_of = {p: n_refs[g][at] for g, group in enumerate(groups) for at, p in enumerate(group)}
    for p in range(panels):
        for s in range(slots):
            at = where[p * slots + s]
            value = total[jnp.maximum(at, 0)]
            panel_ref[p, s] = jnp.where(at >= 0, -value, 0.0)
        diag_ref[p] = lax.dot_general(
            n_of[p].reshape(slots * rb, width),
            panel_ref[p].reshape(slots * rb, width),
            (((0,), (0,)), ((), ())),
            precision=HIGHEST,
            preferred_element_type=jnp.float32,
        )


def on_device(
    lines, inverse_matrix, factor_blocks, factor_inverse, diag_given, block_lists, list_mask, slot_of_block
):
    panels, slots, rb, width = factor_blocks.shape
    halves = inverse_matrix.shape[1] // width
    f32 = jnp.float32
    r = lax.axis_index("prow").astype(jnp.int32)
    col = lax.axis_index("pcol").astype(jnp.int32)
    z, h = col // 2, col % 2
    place = jnp.stack([r, z, h])

    def send(value, to):
        pairs = []
        for a in range(lines):
            for b in range(lines):
                for c in range(2):
                    target = to(a, b, c)
                    if target is not None:
                        ta, tb, tc = target
                        pairs.append(((a * lines + b) * 2 + c, (ta * lines + tb) * 2 + tc))
        return lax.ppermute(value, AXES, pairs)

    def swap(value):
        return send(value, lambda a, b, c: (a, b, 1 - c))

    def across(value, d):
        return send(value, lambda a, b, c: (a ^ d, b, c))

    def along(value, m):
        return send(value, lambda a, b, c: (a, (b + m) % lines, c))

    slot_valid = valid_slots(block_lists, list_mask, slot_of_block)
    row_valid = lax.dynamic_slice_in_dim(slot_valid, r * slots, slots, 1).reshape(panels * slots)
    order = jnp.arange(panels * slots, dtype=jnp.int32)
    before = jnp.sum(jnp.where(order[None, :] < order[:, None], row_valid[None, :], 0), axis=1)
    where = jnp.where(row_valid > 0, before, -1).astype(jnp.int32)

    keep = 3 * panels * slots // 4
    half = panels // 2
    groups = [tuple(range(half)), tuple(range(half, panels))]
    bounds = [0, keep // 2, keep]

    split, normalized, parts_of, planes, stacked, gathered, halved = [], [], [], [], [], [], []

    def normalize(group, after):
        shape = (2, len(group) * halves * rb // lines, width)
        rows_made = jax.ShapeDtypeStruct((len(group), slots, rb, width), f32)
        made = call(
            functools.partial(normalize_kernel, group, lines),
            [rows_made] + [jax.ShapeDtypeStruct(shape, f32)] * lines,
            [pltpu.VMEM((2, len(group) * halves * rb, width), f32)],
            n_scalar=2, n_in=3, n_after=len(after),
            flops=6 * lines * math.prod(shape) * width, moved=8 * lines * math.prod(shape),
        )(place, row_valid, factor_blocks, partner, factor_inverse, *after)
        normalized.append(made[0])
        parts_of.append(made[1:])

    partner = swap(lax.dynamic_slice_in_dim(factor_blocks, (1 - h) * halves, halves, 1))
    spread = []
    for g, group in enumerate(groups):
        normalize(group, spread)
        parts = parts_of[g]
        moved = 8 * lines * math.prod(parts[0].shape)
        held = [parts[0]] + [across(parts[d], d) for d in range(1, lines)]
        outgoing = call(
            functools.partial(to_planes_kernel, lines),
            [jax.ShapeDtypeStruct(parts[0].shape, f32)] * lines, n_in=lines, moved=moved,
        )(place, *held)
        spread = [outgoing[0]]
        planes.append(outgoing)
    along_planes = [
        [outgoing[0]] + [along(outgoing[m], m) for m in range(1, lines)] for outgoing in planes
    ]
    for g, group in enumerate(groups):
        held = along_planes[g]
        shape = held[0].shape
        after = halved[-1:] + ([planes[g + 1][0]] if g + 1 < len(groups) else [])
        [both] = call(
            stack_kernel, [jax.ShapeDtypeStruct((2, lines) + shape[1:], f32)], n_in=lines,
            n_after=len(after), moved=8 * lines * math.prod(shape),
        )(place, *held, *after)
        pieces = [both] + [across(both, d) for d in range(1, lines)]
        if lines == 4:
            half_shape = jax.ShapeDtypeStruct((1,) + both.shape[1:], f32)
            before = along_planes[g + 1][1:] if g + 1 < len(groups) else []
            split_pair = call(
                halves_kernel, [half_shape, half_shape], n_scalar=0, n_in=2,
                n_after=len(before), moved=8 * both.size // 2,
            )(pieces[1], pieces[2], *before)
            pieces[3:] = [across(split_pair[0], 2), across(split_pair[1], 1)]
            halved.append(split_pair[0])
        stacked.append(both)
        gathered.append(pieces)

    def assemble(g, after):
        group, pieces = groups[g], gathered[g]
        block = jax.ShapeDtypeStruct((len(group), halves * width, width), jnp.bfloat16)
        x_hi, x_lo = call(
            functools.partial(assemble_kernel, lines, rb),
            [block, block],
            [pltpu.VMEM((len(group) * halves * width, width), f32)],
            n_in=len(pieces), n_after=len(after), moved=8 * len(group) * halves * width * width,
        )(place, *pieces, *after)
        split.extend((x_hi, x_lo, at) for at in range(len(group)))

    g3 = inverse_matrix.reshape(slots, width, halves * width)
    order = [
        sorted(
            (j for j in range(lines) if j != a),
            key=lambda j: (lines - 1 - j + a, 0) if j > a else (j + lines - 1 - a, 1),
        )
        + [a]
        for a in range(lines)
    ]

    def of_plane(values):
        return sum(jnp.where(z == a, jnp.int32(v), 0) for a, v in enumerate(values))

    def chosen(made, calls):
        kinds = sorted({c for c in calls.values() if c is not None})
        value = made[kinds[-1]][0] + made[kinds[-1]][1]
        for c in kinds[:-1]:
            here = [(z == a) & (h == core) for (a, core), named in calls.items() if named == c]
            here = functools.reduce(jnp.logical_or, here)
            value = jnp.where(here, made[c][0] + made[c][1], value)
        return value

    def add_arrived(value, arrived, step):
        behind = jnp.where(h == 0, z, lines - 1 - z)
        return jnp.where((behind > 0) & (behind <= step + 1), value + arrived, value)

    assemble(0, halved[1:2])
    assemble(1, [])
    made = [[], []]
    moving = [[], []]

    def compute(after):
        n = len(made[0])
        info = jnp.stack([of_plane([order[a][n] for a in range(lines)])])
        for k, terms in enumerate(product(g3, split, bounds, rb, info, where, after)):
            made[k].append((terms, swap(terms) if n < lines - 1 else None))

    def move(k, step):
        calls = {}
        for a in range(lines):
            calls[a, 0] = order[a].index(lines - 1 - step + a) if a <= step else None
            calls[a, 1] = order[a].index(step - lines + 1 + a) if a >= lines - 1 - step else None
        value = chosen(made[k], calls)
        if step:
            value = add_arrived(value, moving[k][-1], step - 1)
        moving[k].append(
            send(value, lambda a, b, c: (a, b + 1 - 2 * c, c) if 0 <= b + 1 - 2 * c < lines else (a, b, 1 - c))
        )
        return [value]

    compute([])
    for step in range(lines - 1):
        after = move(0, step)
        if step == 0:
            compute(after)
            move(1, 0)
            continue
        if step < lines - 2:
            compute(after)
        after = move(1, step)
        if step == lines - 3:
            compute(after)
    made_0, made_1 = made
    moving_0, moving_1 = moving

    half_rows = jax.ShapeDtypeStruct((keep, rb, width), f32)
    mine, other = call(
        functools.partial(merge_kernel, bounds, lines), [half_rows, half_rows], n_in=4, moved=24 * keep * rb * width
    )(place, made_0[-1][0], moving_0[-1], made_1[-1][0], moving_1[-1])
    panel_inverse, terms = call(
        functools.partial(finish_kernel, groups),
        [
            jax.ShapeDtypeStruct(factor_blocks.shape, f32),
            jax.ShapeDtypeStruct(factor_inverse.shape, f32),
        ],
        [pltpu.VMEM((keep, rb, width), f32)],
        n_in=len(groups) + 2, flops=12 * factor_blocks.size * width, moved=20 * factor_blocks.size,
    )(where, *normalized, mine, swap(other))

    pick = lambda value, at: lax.dynamic_index_in_dim(value, at, 0, False)
    two = terms.reshape(2, half * width, width)
    total = pick(two, h) + swap(pick(two, 1 - h))
    parts = total.reshape(lines, -1, width)
    total = pick(parts, r)
    for piece in [across(pick(parts, r ^ d), d) for d in range(1, lines)]:
        total = total + piece
    parts = total.reshape(lines, -1, width)
    total = pick(parts, z)
    for piece in [along(pick(parts, (z + m) % lines), m) for m in range(1, lines)]:
        total = total + piece
    pieces = [total] + [along(total, m) for m in range(1, lines)]
    gathered = jnp.zeros((lines,) + total.shape, f32)
    for m in range(lines):
        gathered = lax.dynamic_update_index_in_dim(gathered, pieces[m], (z - m) % lines, 0)
    total = gathered.reshape(-1, width)
    pieces = [total] + [across(total, d) for d in range(1, lines)]
    gathered = jnp.zeros((lines,) + total.shape, f32)
    for d in range(lines):
        gathered = lax.dynamic_update_index_in_dim(gathered, pieces[d], r ^ d, 0)
    total = gathered.reshape(half, width, width)
    swapped = swap(total)
    summed = jnp.concatenate([jnp.where(h == 0, total, swapped), jnp.where(h == 0, swapped, total)], 0)
    return (panel_inverse, diag_given - summed)


def solution(mesh):
    lines = mesh.shape["prow"]
    if mesh.shape["pcol"] != 2 * lines:
        raise ValueError("mesh shape")
    placed = (P("prow", "pcol"), P(None, "prow", "pcol", None), P(), P(), P(), P(), P())
    return jax.shard_map(
        functools.partial(on_device, lines),
        mesh=mesh,
        in_specs=placed,
        out_specs=(P(None, "prow", "pcol", None), P()),
        check_vma=False,
    )
```

```python
import functools
import math
import jax
import jax.numpy as jnp
from jax import lax
from jax.experimental import pallas as pl
from jax.experimental.pallas import tpu as pltpu
from jax.sharding import PartitionSpec as P

AXES = ("prow", "pcol")
HIGHEST = lax.Precision.HIGHEST
VMEM_LIMIT = 56 * 1024 * 1024


def whole(memory_space=pltpu.VMEM):
    return pl.BlockSpec(memory_space=memory_space)


def call(kernel, outs, scratch=(), n_scalar=1, n_in=1, n_after=0, n_gated=0, flops=0, moved=0):
    used = n_scalar + n_in
    made = len(outs) - n_gated

    def body(*refs):
        rest = refs[used + n_after :]
        kernel(*refs[:used], *rest[:made], *rest[made + n_gated :])

    return pl.pallas_call(
        body,
        out_shape=outs,
        in_specs=[whole(pltpu.SMEM)] * n_scalar + [whole()] * n_in + [whole(pl.ANY)] * n_after,
        out_specs=[whole()] * made + [whole(pl.ANY)] * n_gated,
        input_output_aliases={used + k: made + k for k in range(n_gated)},
        scratch_shapes=list(scratch),
        compiler_params=pltpu.CompilerParams(vmem_limit_bytes=VMEM_LIMIT),
        cost_estimate=pl.CostEstimate(flops=flops, bytes_accessed=moved, transcendentals=0),
    )


def valid_slots(block_lists, list_mask, slot_of_block):
    window_blocks = block_lists.shape[1]
    block_ids = jnp.arange(window_blocks, dtype=jnp.int32)
    chosen = (block_lists[:, :, None] == block_ids[None, None, :]).astype(jnp.int32)
    slot_ids = jnp.sum(chosen * slot_of_block[None, None, :], axis=2)
    matches = (slot_ids[:, :, None] == block_ids[None, None, :]).astype(jnp.int32)
    return jnp.sum(matches * list_mask[:, :, None], axis=1)


def normalize_kernel(group, lines, place, valid, f_ref, partner_ref, inv_ref, n_ref, *rest):
    slots, rb, width = f_ref.shape[1:]
    halves = slots // 2
    outs, scratch = rest[:lines], rest[lines]
    r, h = place[0], place[2]
    rows = halves * rb

    def times(block, p):
        return jnp.dot(block, inv_ref[p], precision=HIGHEST, preferred_element_type=jnp.float32)

    for at, p in enumerate(group):
        block = times(f_ref[p].reshape(slots * rb, width), p)
        for s in range(slots):
            one = block[s * rb : (s + 1) * rb]
            n_ref[at, s] = jnp.where(valid[p * slots + s] > 0, one, 0.0)
        block = times(partner_ref[p].reshape(rows, width), p)
        for t in range(halves):
            one = block[t * rb : (t + 1) * rb]
            row = at * rows + t * rb
            used = valid[p * slots + h * halves + t] > 0
            scratch[1 - h, row : row + rb] = jnp.where(used, one, 0.0)
            scratch[h, row : row + rb] = n_ref[at, h * halves + t]
    n = len(group) * rows // lines
    for d in range(lines):
        start = pl.multiple_of((r ^ d) * n, 8)
        outs[d][...] = scratch[:, pl.ds(start, n), :]


def to_planes_kernel(lines, place, *refs):
    r, z = place[0], place[1]
    for m in range(lines):
        which = r ^ ((z + m) % lines)
        for d in range(lines):

            @pl.when(which == d)
            def _(m=m, d=d):
                refs[lines + m][...] = refs[d][...]


def stack_kernel(place, *refs):
    for m in range(len(refs) - 1):
        refs[-1][:, m] = refs[m][...]


def assemble_kernel(lines, rb, place, *refs):
    pieces, (hi_ref, lo_ref, held) = refs[:-3], refs[-3:]
    r, z = place[0], place[1]
    n, width = pieces[0].shape[2:]
    step = math.gcd(n, rb)
    for d in range(lines):
        line = r ^ d
        for core in range(2):
            if len(pieces) > lines and d == lines - 1:
                piece, at = pieces[d + core], 0
            else:
                piece, at = pieces[d], core
            for m in range(lines):
                plane = (z + lines - m) % lines
                for i in range(n // step):
                    flat = line * n + i * step
                    row = (flat // rb) * width + (plane * 2 + core) * rb + flat % rb
                    row = pl.multiple_of(row, 8)
                    held[pl.ds(row, step), :] = piece[at, m, i * step : (i + 1) * step, :]
    panels, depth, _ = hi_ref.shape

    @pl.loop(0, panels * depth // width)
    def _(i):
        row = pl.multiple_of(i * width, width)
        value = held[pl.ds(row, width), :]
        hi = value.astype(jnp.bfloat16)
        p = row // depth
        at = pl.multiple_of(row % depth, width)
        hi_ref[p, pl.ds(at, width), :] = hi
        lo_ref[p, pl.ds(at, width), :] = (value - hi.astype(jnp.float32)).astype(jnp.bfloat16)


def product_kernel(panels, slots, bounds, waits, info, where, g_ref, *refs):
    x_hi, x_lo = refs[:panels], refs[panels : 2 * panels]
    outs, held, done = refs[2 * panels + waits : -2], refs[-2], refs[-1]
    tile = pl.program_id(0)
    tile_slots, rows, depth = g_ref.shape
    g = g_ref[...].reshape(tile_slots * rows, depth)
    g_hi = g.astype(jnp.bfloat16)
    g_lo = (g - g_hi.astype(jnp.float32)).astype(jnp.bfloat16)
    dot = functools.partial(jnp.dot, preferred_element_type=jnp.float32)
    for p in range(panels):
        value = dot(g_hi, x_hi[p][0]) + (dot(g_hi, x_lo[p][0]) + dot(g_lo, x_hi[p][0]))
        for s in range(tile_slots):
            at = where[p * slots + tile * tile_slots + s]
            held[jnp.where(at >= 0, at, bounds[-1])] = value[s * rows : (s + 1) * rows]

    @pl.when(tile == pl.num_programs(0) - 1)
    def _():
        copies = [
            pltpu.make_async_copy(held.at[pl.ds(bounds[k], bounds[k + 1] - bounds[k])], out, done.at[k])
            for k, out in enumerate(outs)
        ]
        for copy in copies:
            copy.start()
        for copy in copies:
            copy.wait()


def product(g3, xs, bounds, rb, info, where, after):
    slots, width, depth = g3.shape
    columns = xs[0][0].shape[2]
    rows = 2 * rb
    tile_slots = math.gcd(slots, max(1, 256 // rows))
    x_specs = [
        pl.BlockSpec((1, depth, columns), functools.partial(lambda at, a, i, w: (at, 0, 0), at))
        for _, _, at in xs
    ]
    anywhere = pl.BlockSpec(memory_space=pl.ANY)
    pieces = len(bounds) - 1
    return pl.pallas_call(
        functools.partial(product_kernel, len(xs), slots, bounds, len(after)),
        out_shape=[
            jax.ShapeDtypeStruct((bounds[k + 1] - bounds[k], rows, columns), jnp.float32) for k in range(pieces)
        ],
        grid_spec=pltpu.PrefetchScalarGridSpec(
            num_scalar_prefetch=2,
            grid=(slots // tile_slots,),
            in_specs=[pl.BlockSpec((tile_slots, rows, depth), lambda tile, i, w: (tile, i[0], 0))]
            + x_specs + x_specs + [anywhere] * len(after),
            out_specs=[anywhere] * pieces,
            scratch_shapes=[
                pltpu.VMEM((bounds[-1] + 1, rows, columns), jnp.float32),
                pltpu.SemaphoreType.DMA((pieces,)),
            ],
        ),
        compiler_params=pltpu.CompilerParams(vmem_limit_bytes=VMEM_LIMIT),
        cost_estimate=pl.CostEstimate(
            flops=12 * slots * rows * depth * columns * len(xs),
            bytes_accessed=slots * rows * depth * 4, transcendentals=0,
        ),
    )(info, where, g3, *[x[0] for x in xs], *[x[1] for x in xs], *after)


def merge_kernel(lines, place, own_ref, arrived_ref, mine, other):
    rb = mine.shape[1]
    from_others = place[1] != jnp.where(place[2] == 0, 0, lines - 1)
    for core in range(2):
        rows = slice(core * rb, (core + 1) * rb)

        def fill(out, rows=rows):
            out[...] = own_ref[:, rows, :] + jnp.where(from_others, arrived_ref[:, rows, :], 0.0)

        pl.when(place[2] == core)(functools.partial(fill, mine))
        pl.when(place[2] != core)(functools.partial(fill, other))


def finish_kernel(groups, bounds, where, *refs):
    n_refs, refs = refs[: len(groups)], refs[len(groups) :]
    panel_ref, diag_ref, total = refs[-3:]
    for k in range(len(bounds) - 1):
        total[bounds[k] : bounds[k + 1]] = refs[2 * k][...] + refs[2 * k + 1][...]
    panels, slots, rb, width = panel_ref.shape
    n_of = {p: n_refs[g][at] for g, group in enumerate(groups) for at, p in enumerate(group)}
    for p in range(panels):
        for s in range(slots):
            at = where[p * slots + s]
            value = total[jnp.maximum(at, 0)]
            panel_ref[p, s] = jnp.where(at >= 0, -value, 0.0)
        diag_ref[p] = lax.dot_general(
            n_of[p].reshape(slots * rb, width),
            panel_ref[p].reshape(slots * rb, width),
            (((0,), (0,)), ((), ())),
            precision=HIGHEST,
            preferred_element_type=jnp.float32,
        )


def on_device(
    lines, inverse_matrix, factor_blocks, factor_inverse, diag_given, block_lists, list_mask, slot_of_block
):
    panels, slots, rb, width = factor_blocks.shape
    halves = inverse_matrix.shape[1] // width
    f32 = jnp.float32
    r = lax.axis_index("prow").astype(jnp.int32)
    col = lax.axis_index("pcol").astype(jnp.int32)
    z, h = col // 2, col % 2
    place = jnp.stack([r, z, h])

    def send(value, to):
        pairs = []
        for a in range(lines):
            for b in range(lines):
                for c in range(2):
                    target = to(a, b, c)
                    if target is not None:
                        ta, tb, tc = target
                        pairs.append(((a * lines + b) * 2 + c, (ta * lines + tb) * 2 + tc))
        return lax.ppermute(value, AXES, pairs)

    def swap(value):
        return send(value, lambda a, b, c: (a, b, 1 - c))

    def across(value, d):
        return send(value, lambda a, b, c: (a ^ d, b, c))

    def along(value, m):
        return send(value, lambda a, b, c: (a, (b + m) % lines, c))

    slot_valid = valid_slots(block_lists, list_mask, slot_of_block)
    row_valid = lax.dynamic_slice_in_dim(slot_valid, r * slots, slots, 1).reshape(panels * slots)
    order = jnp.arange(panels * slots, dtype=jnp.int32)
    before = jnp.sum(jnp.where(order[None, :] < order[:, None], row_valid[None, :], 0), axis=1)
    where = jnp.where(row_valid > 0, before, -1).astype(jnp.int32)

    keep = 3 * panels * slots // 4
    half = panels // 2
    groups = [tuple(range(half)), tuple(range(half, panels))]
    bounds = [0, keep // 2, keep]

    split, normalized, parts_of, planes, stacked, gathered, halved = [], [], [], [], [], [], []

    def normalize(group, after):
        shape = (2, len(group) * halves * rb // lines, width)
        rows_made = jax.ShapeDtypeStruct((len(group), slots, rb, width), f32)
        made = call(
            functools.partial(normalize_kernel, group, lines),
            [rows_made] + [jax.ShapeDtypeStruct(shape, f32)] * lines,
            [pltpu.VMEM((2, len(group) * halves * rb, width), f32)],
            n_scalar=2, n_in=3, n_after=len(after),
            flops=6 * lines * math.prod(shape) * width, moved=8 * lines * math.prod(shape),
        )(place, row_valid, factor_blocks, partner, factor_inverse, *after)
        normalized.append(made[0])
        parts_of.append(made[1:])

    partner = swap(lax.dynamic_slice_in_dim(factor_blocks, (1 - h) * halves, halves, 1))
    for g, group in enumerate(groups):
        normalize(group, normalized[-1:])
    for g, group in enumerate(groups):
        parts = parts_of[g]
        part = jax.ShapeDtypeStruct(parts[0].shape, f32)
        held = [parts[0]] + [across(parts[d], d) for d in range(1, lines)]
        gated = parts_of[g + 1] if g + 1 < len(groups) else []
        outgoing = call(
            functools.partial(to_planes_kernel, lines),
            [part] * lines + [jax.ShapeDtypeStruct(v.shape, f32) for v in gated],
            n_in=lines, n_after=len(gated), n_gated=len(gated), moved=8 * lines * parts[0].size,
        )(place, *held, *gated)
        planes.append(outgoing[:lines])
        if gated:
            parts_of[g + 1] = outgoing[lines:]

    along_planes = [
        [outgoing[0]] + [along(outgoing[m], m) for m in range(1, lines)] for outgoing in planes
    ]
    for g, group in enumerate(groups):
        held = along_planes[g]
        shape = held[0].shape
        after = halved[-1:] + ([planes[g + 1][0]] if g + 1 < len(groups) else [])
        [both] = call(
            stack_kernel, [jax.ShapeDtypeStruct((2, lines) + shape[1:], f32)], n_in=lines,
            n_after=len(after), moved=8 * lines * math.prod(shape),
        )(place, *held, *after)
        pieces = [both] + [across(both, d) for d in range(1, lines)]
        if lines == 4:
            pieces[3:] = [across(pieces[1][:1], 2), across(pieces[2][1:], 1)]
        halved.append(pieces[1])
        stacked.append(both)
        gathered.append(pieces)

    def assemble(g, after):
        group, pieces = groups[g], gathered[g]
        block = jax.ShapeDtypeStruct((len(group), halves * width, width), jnp.bfloat16)
        x_hi, x_lo = call(
            functools.partial(assemble_kernel, lines, rb),
            [block, block],
            [pltpu.VMEM((len(group) * halves * width, width), f32)],
            n_in=len(pieces), n_after=len(after), moved=8 * len(group) * halves * width * width,
        )(place, *pieces, *after)
        split.extend((x_hi, x_lo, at) for at in range(len(group)))

    g3 = inverse_matrix.reshape(slots, width, halves * width)
    order = [
        sorted(
            (j for j in range(lines) if j != a),
            key=lambda j: (lines - 1 - j + a, 0) if j > a else (j + lines - 1 - a, 1),
        )
        + [a]
        for a in range(lines)
    ]

    def of_plane(values):
        return sum(jnp.where(z == a, jnp.int32(v), 0) for a, v in enumerate(values))

    def chosen(made, calls):
        kinds = sorted({c for c in calls.values() if c is not None})
        value = made[kinds[-1]][0] + made[kinds[-1]][1]
        for c in kinds[:-1]:
            here = [(z == a) & (h == core) for (a, core), named in calls.items() if named == c]
            here = functools.reduce(jnp.logical_or, here)
            value = jnp.where(here, made[c][0] + made[c][1], value)
        return value

    def add_arrived(value, arrived, step):
        behind = jnp.where(h == 0, z, lines - 1 - z)
        return jnp.where((behind > 0) & (behind <= step + 1), value + arrived, value)

    assemble(0, halved[1:2])
    assemble(1, [])
    made = [[], []]
    moving = [[], []]

    def compute(after):
        n = len(made[0])
        info = jnp.stack([of_plane([order[a][n] for a in range(lines)])])
        for k, terms in enumerate(product(g3, split, bounds, rb, info, where, after)):
            made[k].append((terms, swap(terms) if n < lines - 1 else None))

    def move(k, step):
        calls = {}
        for a in range(lines):
            calls[a, 0] = order[a].index(lines - 1 - step + a) if a <= step else None
            calls[a, 1] = order[a].index(step - lines + 1 + a) if a >= lines - 1 - step else None
        value = chosen(made[k], calls)
        if step:
            value = add_arrived(value, moving[k][-1], step - 1)
        moving[k].append(
            send(value, lambda a, b, c: (a, b + 1 - 2 * c, c) if 0 <= b + 1 - 2 * c < lines else (a, b, 1 - c))
        )
        return [value]

    compute([])
    for step in range(lines - 1):
        after = move(0, step)
        if step == 0:
            compute(after)
            move(1, 0)
            continue
        if step < lines - 2:
            compute(after)
        after = move(1, step)
        if step == lines - 3:
            compute(after)
    finals = []
    for k in range(2):
        half_rows = jax.ShapeDtypeStruct((bounds[k + 1] - bounds[k], rb, width), f32)
        mine, other = call(
            functools.partial(merge_kernel, lines), [half_rows, half_rows], n_in=2, moved=12 * keep * rb * width
        )(place, made[k][-1][0], moving[k][-1])
        finals += [mine, swap(other)]
    panel_inverse, terms = call(
        functools.partial(finish_kernel, groups, bounds),
        [
            jax.ShapeDtypeStruct(factor_blocks.shape, f32),
            jax.ShapeDtypeStruct(factor_inverse.shape, f32),
        ],
        [pltpu.VMEM((keep, rb, width), f32)],
        n_in=len(groups) + len(finals), flops=12 * factor_blocks.size * width, moved=20 * factor_blocks.size,
    )(where, *normalized, *finals)

    pick = lambda value, at: lax.dynamic_index_in_dim(value, at, 0, False)
    two = terms.reshape(2, half * width, width)
    total = pick(two, h) + swap(pick(two, 1 - h))
    parts = total.reshape(lines, -1, width)
    total = pick(parts, r)
    for piece in [across(pick(parts, r ^ d), d) for d in range(1, lines)]:
        total = total + piece
    parts = total.reshape(lines, -1, width)
    total = pick(parts, z)
    for piece in [along(pick(parts, (z + m) % lines), m) for m in range(1, lines)]:
        total = total + piece
    pieces = [total] + [along(total, m) for m in range(1, lines)]
    gathered = jnp.zeros((lines,) + total.shape, f32)
    for m in range(lines):
        gathered = lax.dynamic_update_index_in_dim(gathered, pieces[m], (z - m) % lines, 0)
    total = gathered.reshape(-1, width)
    pieces = [total] + [across(total, d) for d in range(1, lines)]
    gathered = jnp.zeros((lines,) + total.shape, f32)
    for d in range(lines):
        gathered = lax.dynamic_update_index_in_dim(gathered, pieces[d], r ^ d, 0)
    total = gathered.reshape(half, width, width)
    swapped = swap(total)
    summed = jnp.concatenate([jnp.where(h == 0, total, swapped), jnp.where(h == 0, swapped, total)], 0)
    return (panel_inverse, diag_given - summed)


def solution(mesh):
    lines = mesh.shape["prow"]
    if mesh.shape["pcol"] != 2 * lines:
        raise ValueError("mesh shape")
    placed = (P("prow", "pcol"), P(None, "prow", "pcol", None), P(), P(), P(), P(), P())
    return jax.shard_map(
        functools.partial(on_device, lines),
        mesh=mesh,
        in_specs=placed,
        out_specs=(P(None, "prow", "pcol", None), P()),
        check_vma=False,
    )
```

```python
import functools
import math
import jax
import jax.numpy as jnp
from jax import lax
from jax.experimental import pallas as pl
from jax.experimental.pallas import tpu as pltpu
from jax.sharding import PartitionSpec as P

AXES = ("prow", "pcol")
HIGHEST = lax.Precision.HIGHEST
VMEM_LIMIT = 56 * 1024 * 1024


def whole(memory_space=pltpu.VMEM):
    return pl.BlockSpec(memory_space=memory_space)


def call(kernel, outs, scratch=(), n_scalar=1, n_in=1, n_after=0, n_gated=0, flops=0, moved=0):
    used = n_scalar + n_in
    made = len(outs) - n_gated

    def body(*refs):
        rest = refs[used + n_after :]
        kernel(*refs[:used], *rest[:made], *rest[made + n_gated :])

    return pl.pallas_call(
        body,
        out_shape=outs,
        in_specs=[whole(pltpu.SMEM)] * n_scalar + [whole()] * n_in + [whole(pl.ANY)] * n_after,
        out_specs=[whole()] * made + [whole(pl.ANY)] * n_gated,
        input_output_aliases={used + k: made + k for k in range(n_gated)},
        scratch_shapes=list(scratch),
        compiler_params=pltpu.CompilerParams(vmem_limit_bytes=VMEM_LIMIT),
        cost_estimate=pl.CostEstimate(flops=flops, bytes_accessed=moved, transcendentals=0),
    )


def valid_slots(block_lists, list_mask, slot_of_block):
    window_blocks = block_lists.shape[1]
    block_ids = jnp.arange(window_blocks, dtype=jnp.int32)
    chosen = (block_lists[:, :, None] == block_ids[None, None, :]).astype(jnp.int32)
    slot_ids = jnp.sum(chosen * slot_of_block[None, None, :], axis=2)
    matches = (slot_ids[:, :, None] == block_ids[None, None, :]).astype(jnp.int32)
    return jnp.sum(matches * list_mask[:, :, None], axis=1)


def normalize_kernel(group, lines, place, valid, f_ref, partner_ref, inv_ref, n_ref, *rest):
    slots, rb, width = f_ref.shape[1:]
    halves = slots // 2
    outs, scratch = rest[:lines], rest[lines]
    r, h = place[0], place[2]
    rows = halves * rb

    def times(block, p):
        return jnp.dot(block, inv_ref[p], precision=HIGHEST, preferred_element_type=jnp.float32)

    for at, p in enumerate(group):
        block = times(f_ref[p].reshape(slots * rb, width), p)
        for s in range(slots):
            one = block[s * rb : (s + 1) * rb]
            n_ref[at, s] = jnp.where(valid[p * slots + s] > 0, one, 0.0)
        block = times(partner_ref[p].reshape(rows, width), p)
        for t in range(halves):
            one = block[t * rb : (t + 1) * rb]
            row = at * rows + t * rb
            used = valid[p * slots + h * halves + t] > 0
            scratch[1 - h, row : row + rb] = jnp.where(used, one, 0.0)
            scratch[h, row : row + rb] = n_ref[at, h * halves + t]
    n = len(group) * rows // lines
    for d in range(lines):
        start = pl.multiple_of((r ^ d) * n, 8)
        outs[d][...] = scratch[:, pl.ds(start, n), :]


def to_planes_kernel(lines, place, *refs):
    r, z = place[0], place[1]
    for m in range(lines):
        which = r ^ ((z + m) % lines)
        for d in range(lines):

            @pl.when(which == d)
            def _(m=m, d=d):
                refs[lines + m][...] = refs[d][...]


def stack_kernel(place, *refs):
    for m in range(len(refs) - 1):
        refs[-1][:, m] = refs[m][...]


def assemble_kernel(lines, rb, place, *refs):
    pieces, (hi_ref, lo_ref, held) = refs[:-3], refs[-3:]
    r, z = place[0], place[1]
    n, width = pieces[0].shape[2:]
    step = math.gcd(n, rb)
    for d in range(lines):
        line = r ^ d
        for core in range(2):
            if len(pieces) > lines and d == lines - 1:
                piece, at = pieces[d + core], 0
            else:
                piece, at = pieces[d], core
            for m in range(lines):
                plane = (z + lines - m) % lines
                for i in range(n // step):
                    flat = line * n + i * step
                    row = (flat // rb) * width + (plane * 2 + core) * rb + flat % rb
                    row = pl.multiple_of(row, 8)
                    held[pl.ds(row, step), :] = piece[at, m, i * step : (i + 1) * step, :]
    panels, depth, _ = hi_ref.shape

    @pl.loop(0, panels * depth // width)
    def _(i):
        row = pl.multiple_of(i * width, width)
        value = held[pl.ds(row, width), :]
        hi = value.astype(jnp.bfloat16)
        p = row // depth
        at = pl.multiple_of(row % depth, width)
        hi_ref[p, pl.ds(at, width), :] = hi
        lo_ref[p, pl.ds(at, width), :] = (value - hi.astype(jnp.float32)).astype(jnp.bfloat16)


def product_kernel(panels, slots, bounds, waits, info, where, g_ref, *refs):
    x_hi, x_lo = refs[:panels], refs[panels : 2 * panels]
    outs, held, done = refs[2 * panels + waits : -2], refs[-2], refs[-1]
    tile = pl.program_id(0)
    tile_slots, rows, depth = g_ref.shape
    g = g_ref[...].reshape(tile_slots * rows, depth)
    g_hi = g.astype(jnp.bfloat16)
    g_lo = (g - g_hi.astype(jnp.float32)).astype(jnp.bfloat16)
    dot = functools.partial(jnp.dot, preferred_element_type=jnp.float32)
    for p in range(panels):
        value = dot(g_hi, x_hi[p][0]) + (dot(g_hi, x_lo[p][0]) + dot(g_lo, x_hi[p][0]))
        for s in range(tile_slots):
            at = where[p * slots + tile * tile_slots + s]
            held[jnp.where(at >= 0, at, bounds[-1])] = value[s * rows : (s + 1) * rows]

    @pl.when(tile == pl.num_programs(0) - 1)
    def _():
        copies = [
            pltpu.make_async_copy(held.at[pl.ds(bounds[k], bounds[k + 1] - bounds[k])], out, done.at[k])
            for k, out in enumerate(outs)
        ]
        for copy in copies:
            copy.start()
        for copy in copies:
            copy.wait()


def product(g3, xs, bounds, rb, info, where, after):
    slots, width, depth = g3.shape
    columns = xs[0][0].shape[2]
    rows = 2 * rb
    tile_slots = math.gcd(slots, max(1, 256 // rows))
    x_specs = [
        pl.BlockSpec((1, depth, columns), functools.partial(lambda at, a, i, w: (at, 0, 0), at))
        for _, _, at in xs
    ]
    anywhere = pl.BlockSpec(memory_space=pl.ANY)
    pieces = len(bounds) - 1
    return pl.pallas_call(
        functools.partial(product_kernel, len(xs), slots, bounds, len(after)),
        out_shape=[
            jax.ShapeDtypeStruct((bounds[k + 1] - bounds[k], rows, columns), jnp.float32) for k in range(pieces)
        ],
        grid_spec=pltpu.PrefetchScalarGridSpec(
            num_scalar_prefetch=2,
            grid=(slots // tile_slots,),
            in_specs=[pl.BlockSpec((tile_slots, rows, depth), lambda tile, i, w: (tile, i[0], 0))]
            + x_specs + x_specs + [anywhere] * len(after),
            out_specs=[anywhere] * pieces,
            scratch_shapes=[
                pltpu.VMEM((bounds[-1] + 1, rows, columns), jnp.float32),
                pltpu.SemaphoreType.DMA((pieces,)),
            ],
        ),
        compiler_params=pltpu.CompilerParams(vmem_limit_bytes=VMEM_LIMIT),
        cost_estimate=pl.CostEstimate(
            flops=12 * slots * rows * depth * columns * len(xs),
            bytes_accessed=slots * rows * depth * 4, transcendentals=0,
        ),
    )(info, where, g3, *[x[0] for x in xs], *[x[1] for x in xs], *after)


def finish_kernel(groups, bounds, lines, place, where, *refs):
    from_others = place[1] != jnp.where(place[2] == 0, lines - 1, 0)
    n_refs, refs = refs[: len(groups)], refs[len(groups) :]
    panel_ref, diag_mine, diag_other, total, diag_ref = refs[-5:]
    for k in range(len(bounds) - 1):
        total[bounds[k] : bounds[k + 1]] = refs[2 * k][...] + jnp.where(from_others, refs[2 * k + 1][...], 0.0)
    panels, slots, rb, width = panel_ref.shape
    n_of = {p: n_refs[g][at] for g, group in enumerate(groups) for at, p in enumerate(group)}
    for p in range(panels):
        for s in range(slots):
            at = where[p * slots + s]
            value = total[jnp.maximum(at, 0)]
            panel_ref[p, s] = jnp.where(at >= 0, -value, 0.0)
        diag_ref[p] = lax.dot_general(
            n_of[p].reshape(slots * rb, width),
            panel_ref[p].reshape(slots * rb, width),
            (((0,), (0,)), ((), ())),
            precision=HIGHEST,
            preferred_element_type=jnp.float32,
        )
    half = diag_mine.shape[0]
    diag_mine[...] = diag_ref[pl.ds(place[2] * half, half)]
    diag_other[...] = diag_ref[pl.ds((1 - place[2]) * half, half)]


def on_device(
    lines, inverse_matrix, factor_blocks, factor_inverse, diag_given, block_lists, list_mask, slot_of_block
):
    panels, slots, rb, width = factor_blocks.shape
    halves = inverse_matrix.shape[1] // width
    f32 = jnp.float32
    r = lax.axis_index("prow").astype(jnp.int32)
    col = lax.axis_index("pcol").astype(jnp.int32)
    z, h = col // 2, col % 2
    place = jnp.stack([r, z, h])

    def send(value, to):
        pairs = []
        for a in range(lines):
            for b in range(lines):
                for c in range(2):
                    target = to(a, b, c)
                    if target is not None:
                        ta, tb, tc = target
                        pairs.append(((a * lines + b) * 2 + c, (ta * lines + tb) * 2 + tc))
        return lax.ppermute(value, AXES, pairs)

    def swap(value):
        return send(value, lambda a, b, c: (a, b, 1 - c))

    def across(value, d):
        return send(value, lambda a, b, c: (a ^ d, b, c))

    def along(value, m):
        return send(value, lambda a, b, c: (a, (b + m) % lines, c))

    slot_valid = valid_slots(block_lists, list_mask, slot_of_block)
    row_valid = lax.dynamic_slice_in_dim(slot_valid, r * slots, slots, 1).reshape(panels * slots)
    order = jnp.arange(panels * slots, dtype=jnp.int32)
    before = jnp.sum(jnp.where(order[None, :] < order[:, None], row_valid[None, :], 0), axis=1)
    where = jnp.where(row_valid > 0, before, -1).astype(jnp.int32)

    keep = 3 * panels * slots // 4
    half = panels // 2
    groups = [tuple(range(half)), tuple(range(half, panels))]
    bounds = [0, keep // 2, keep]

    split, normalized, parts_of, planes, stacked, gathered, halved = [], [], [], [], [], [], []

    def normalize(group, after):
        shape = (2, len(group) * halves * rb // lines, width)
        rows_made = jax.ShapeDtypeStruct((len(group), slots, rb, width), f32)
        made = call(
            functools.partial(normalize_kernel, group, lines),
            [rows_made] + [jax.ShapeDtypeStruct(shape, f32)] * lines,
            [pltpu.VMEM((2, len(group) * halves * rb, width), f32)],
            n_scalar=2, n_in=3, n_after=len(after),
            flops=6 * lines * math.prod(shape) * width, moved=8 * lines * math.prod(shape),
        )(place, row_valid, factor_blocks, partner, factor_inverse, *after)
        normalized.append(made[0])
        parts_of.append(made[1:])

    partner = swap(lax.dynamic_slice_in_dim(factor_blocks, (1 - h) * halves, halves, 1))
    for g, group in enumerate(groups):
        normalize(group, normalized[-1:])
    for g, group in enumerate(groups):
        parts = parts_of[g]
        part = jax.ShapeDtypeStruct(parts[0].shape, f32)
        held = [parts[0]] + [across(parts[d], d) for d in range(1, lines)]
        gated = parts_of[g + 1] if g + 1 < len(groups) else []
        outgoing = call(
            functools.partial(to_planes_kernel, lines),
            [part] * lines + [jax.ShapeDtypeStruct(v.shape, f32) for v in gated],
            n_in=lines, n_after=len(gated), n_gated=len(gated), moved=8 * lines * parts[0].size,
        )(place, *held, *gated)
        planes.append(outgoing[:lines])
        if gated:
            parts_of[g + 1] = outgoing[lines:]

    along_planes = [
        [outgoing[0]] + [along(outgoing[m], m) for m in range(1, lines)] for outgoing in planes
    ]
    for g, group in enumerate(groups):
        held = along_planes[g]
        shape = held[0].shape
        after = halved[-1:] + ([planes[g + 1][0]] if g + 1 < len(groups) else [])
        [both] = call(
            stack_kernel, [jax.ShapeDtypeStruct((2, lines) + shape[1:], f32)], n_in=lines,
            n_after=len(after), moved=8 * lines * math.prod(shape),
        )(place, *held, *after)
        pieces = [both] + [across(both, d) for d in range(1, lines)]
        if lines == 4:
            pieces[3:] = [across(pieces[1][:1], 2), across(pieces[2][1:], 1)]
        halved.append(pieces[1])
        stacked.append(both)
        gathered.append(pieces)

    def assemble(g, after):
        group, pieces = groups[g], gathered[g]
        block = jax.ShapeDtypeStruct((len(group), halves * width, width), jnp.bfloat16)
        x_hi, x_lo = call(
            functools.partial(assemble_kernel, lines, rb),
            [block, block],
            [pltpu.VMEM((len(group) * halves * width, width), f32)],
            n_in=len(pieces), n_after=len(after), moved=8 * len(group) * halves * width * width,
        )(place, *pieces, *after)
        split.extend((x_hi, x_lo, at) for at in range(len(group)))

    g3 = inverse_matrix.reshape(slots, width, halves * width)
    order = [
        sorted(
            (j for j in range(lines) if j != a),
            key=lambda j: (lines - 1 - j + a, 0) if j > a else (j + lines - 1 - a, 1),
        )
        + [a]
        for a in range(lines)
    ]

    def of_plane(values):
        return sum(jnp.where(z == a, jnp.int32(v), 0) for a, v in enumerate(values))

    def chosen(made, calls):
        kinds = sorted({c for c in calls.values() if c is not None})
        value = made[kinds[-1]][0] + made[kinds[-1]][1]
        for c in kinds[:-1]:
            here = [(z == a) & (h == core) for (a, core), named in calls.items() if named == c]
            here = functools.reduce(jnp.logical_or, here)
            value = jnp.where(here, made[c][0] + made[c][1], value)
        return value

    def add_arrived(value, arrived, step):
        behind = jnp.where(h == 0, z, lines - 1 - z)
        return jnp.where((behind > 0) & (behind <= step + 1), value + arrived, value)

    assemble(0, halved[1:2])
    assemble(1, [])
    made = [[], []]
    moving = [[], []]

    def compute(after):
        n = len(made[0])
        info = jnp.stack([of_plane([order[a][n] for a in range(lines)])])
        for k, terms in enumerate(product(g3, split, bounds, rb, info, where, after)):
            made[k].append((terms, swap(terms) if n < lines - 1 else None))

    def move(k, step):
        calls = {}
        for a in range(lines):
            calls[a, 0] = order[a].index(lines - 1 - step + a) if a <= step else None
            calls[a, 1] = order[a].index(step - lines + 1 + a) if a >= lines - 1 - step else None
        value = chosen(made[k], calls)
        if step:
            value = add_arrived(value, moving[k][-1], step - 1)
        moving[k].append(
            send(value, lambda a, b, c: (a, b + 1 - 2 * c, c) if 0 <= b + 1 - 2 * c < lines else (a, b, 1 - c))
        )
        return [value]

    compute([])
    for step in range(lines - 1):
        after = move(0, step)
        if step == 0:
            compute(after)
            move(1, 0)
            continue
        if step < lines - 2:
            compute(after)
        after = move(1, step)
        if step == lines - 3:
            compute(after)
    finals = []
    from_others = z != jnp.where(h == 0, 0, lines - 1)
    rows_of = lambda value, core: lax.dynamic_slice_in_dim(value, core * rb, rb, 1)
    for k in range(2):
        own, arrived = made[k][-1][0], moving[k][-1]
        own = rows_of(own, h) + swap(rows_of(own, 1 - h))
        swapped = swap(rows_of(arrived, 1 - h))
        finals += [own + jnp.where(from_others, rows_of(arrived, h), 0.0), swapped]
    diag_half = jax.ShapeDtypeStruct((half, width, width), f32)
    panel_inverse, mine, other = call(
        functools.partial(finish_kernel, groups, bounds, lines),
        [
            jax.ShapeDtypeStruct(factor_blocks.shape, f32),
            diag_half, diag_half,
        ],
        [pltpu.VMEM((keep, rb, width), f32), pltpu.VMEM(factor_inverse.shape, f32)],
        n_scalar=2, n_in=len(groups) + len(finals), flops=12 * factor_blocks.size * width, moved=20 * factor_blocks.size,
    )(place, where, *normalized, *finals)

    pick = lambda value, at: lax.dynamic_index_in_dim(value, at, 0, False)
    total = (mine + swap(other)).reshape(half * width, width)
    parts = total.reshape(lines, -1, width)
    total = pick(parts, r)
    for piece in [across(pick(parts, r ^ d), d) for d in range(1, lines)]:
        total = total + piece
    parts = total.reshape(lines, -1, width)
    total = pick(parts, z)
    for piece in [along(pick(parts, (z + m) % lines), m) for m in range(1, lines)]:
        total = total + piece
    pieces = [total] + [along(total, m) for m in range(1, lines)]
    gathered = jnp.zeros((lines,) + total.shape, f32)
    for m in range(lines):
        gathered = lax.dynamic_update_index_in_dim(gathered, pieces[m], (z - m) % lines, 0)
    total = gathered.reshape(-1, width)
    pieces = [total] + [across(total, d) for d in range(1, lines)]
    gathered = jnp.zeros((lines,) + total.shape, f32)
    for d in range(lines):
        gathered = lax.dynamic_update_index_in_dim(gathered, pieces[d], r ^ d, 0)
    total = gathered.reshape(half, width, width)
    swapped = swap(total)
    summed = jnp.concatenate([jnp.where(h == 0, total, swapped), jnp.where(h == 0, swapped, total)], 0)
    return (panel_inverse, diag_given - summed)


def solution(mesh):
    lines = mesh.shape["prow"]
    if mesh.shape["pcol"] != 2 * lines:
        raise ValueError("mesh shape")
    placed = (P("prow", "pcol"), P(None, "prow", "pcol", None), P(), P(), P(), P(), P())
    return jax.shard_map(
        functools.partial(on_device, lines),
        mesh=mesh,
        in_specs=placed,
        out_specs=(P(None, "prow", "pcol", None), P()),
        check_vma=False,
    )
```
